512 devices in a mesh: dp: 4 (over y_lo), seq: 16 (over x, y_hi, core), tensor: 8 (over z).
Axes of the slice: x: 4, y: 8 (y_hi: 2, y_lo: 4; y = y_hi * 4 + y_lo), z: 8, core: 2. Of those that a mesh axis runs over, the one named last changes fastest.
Arguments:
- tokens: bfloat16 [4096, 4096], P(('dp', 'seq')), parts along dimension 0, may hold values from -6 to 6
- gate_codes: bfloat16 [14336, 4096], P(('seq', 'tensor')), may hold values from -8 to 7, as said below
- gate_scales: float32 [14336, 32], P(('seq', 'tensor')), may hold values from 0.00125 to 0.00625
- up_codes: bfloat16 [14336, 4096], P(('seq', 'tensor')), may hold values from -8 to 7, as said below
- up_scales: float32 [14336, 32], P(('seq', 'tensor')), may hold values from 0.00125 to 0.00625
- down_codes: bfloat16 [14336, 4096], P('seq', 'tensor'), may hold values from -8 to 7, as said below
- down_scales: float32 [112, 4096], P('seq', 'tensor'), may hold values from 0.0006681531 to 0.0033407656
Outputs:
- output: bfloat16 [4096, 4096], P(('dp', 'seq'), 'tensor'), parts along dimension 0
The draws below stay inside these ranges and needn't reach their ends.
There are 4 independent parts, one for each index of `dp`. The reference program is written for one: setup_inputs(seed, part) draws one part's arguments, and reference() takes and returns one part's arrays. A program takes and returns all parts, laid end to end along the dimension named above; an argument that names none is the same for every part. Nothing has to cross between parts.
Inputs may be any that keep to these rules, and one draw needn't show every extreme that they name: `gate_codes`: whole numbers. `up_codes`: whole numbers. `down_codes`: whole numbers.
All inputs are finite; a program needn't handle non-finite values.
Results may differ from the reference program's by a relative error of at most 0.0076.
Values may be sent and summed in bfloat16 or wider, within the bound.
A program may use at most 64 MiB of HBM per device.

```python
import math
import jax
import jax.numpy as jnp
import numpy as np
from jax import lax

D = 4096
WALSH = 512
GROUP = 128
FF = 14336
TOKENS = 1024


def integer_codes(key, row_total, col_total):
    drawn = jax.random.randint(key, (row_total, col_total), -8, 8)
    return drawn.astype(jnp.float32).astype(jnp.bfloat16)


def draw_gate_codes(key, part):
    key = jax.random.fold_in(key, 11)
    return integer_codes(key, FF, D)


def draw_up_codes(key, part):
    key = jax.random.fold_in(key, 23)
    return integer_codes(key, FF, D)


def draw_down_codes(key, part):
    key = jax.random.fold_in(key, 37)
    return integer_codes(key, FF, D)


def levels(rng, shape, shards, low, high):
    factor_of, own = 1.0, jax.random.fold_in(rng, 6)
    for position, blocks in shards:
        steps = jnp.exp(jax.random.uniform(jax.random.fold_in(own, position), (blocks,), jnp.float32, low / len(shards), high / len(shards)))
        factor_of = factor_of * jnp.repeat(steps, shape[position] // blocks).reshape([-1 if axis == position else 1 for axis in range(len(shape))])
    return factor_of


def centred(key, extent, deviation, reach, cuts=(), held_as=jnp.bfloat16):
    values = deviation * jax.random.normal(key, extent, jnp.float32)
    if cuts:
        values = values * levels(key, extent, cuts, -0.22, 0.18)
    return jnp.clip(values, -reach, reach).astype(held_as)


def setup_inputs(seed: int = 0, part: int = 0) -> dict:
    key_of = jax.random.split(jax.random.key(seed), 8)
    part_splits = jax.random.split(jax.random.fold_in(key_of[7], part), 8)
    tokens = centred(part_splits[0], (TOKENS, D), 1.0, 6.0, ((0, 16),))
    gate_codes = draw_gate_codes(jax.random.fold_in(key_of[7], 71), part)
    gate_scales = jnp.clip(jnp.exp(math.log(0.00625) - 1.609438 * jax.random.uniform(key_of[2], (FF, D // GROUP), jnp.float32) ** levels(key_of[2], (FF, D // GROUP), ((0, 128),), -0.2, 0.2)), 0.00125, 0.00625)
    up_codes = draw_up_codes(jax.random.fold_in(key_of[7], 71), part)
    up_scales = jnp.clip(jnp.exp(math.log(0.00625) - 1.609438 * jax.random.uniform(key_of[4], (FF, D // GROUP), jnp.float32) ** levels(key_of[4], (FF, D // GROUP), ((0, 128),), -0.2, 0.2)), 0.00125, 0.00625)
    down_codes = draw_down_codes(jax.random.fold_in(key_of[7], 71), part)
    down_scales = jnp.clip(jnp.exp(math.log(0.0033407656) - 1.609438 * jax.random.uniform(key_of[6], (FF // GROUP, D), jnp.float32) ** levels(key_of[6], (FF // GROUP, D), ((0, 16), (1, 8)), -0.2, 0.2)), 0.0006681531, 0.0033407656)
    return dict(tokens=tokens, gate_codes=gate_codes, gate_scales=gate_scales, up_codes=up_codes, up_scales=up_scales, down_codes=down_codes, down_scales=down_scales)


def sylvester(table_order):
    result_table = jnp.ones((1, 1), jnp.float32)
    kernel_two = jnp.array([[1.0, 1.0], [1.0, -1.0]], jnp.float32)
    while result_table.shape[0] < table_order:
        result_table = jnp.kron(kernel_two, result_table)
    return result_table / jnp.sqrt(jnp.float32(table_order))

def paley_table():
    squares_mod = set((value * value % 13 for value in range(1, 13)))
    conference = np.zeros((14, 14))
    conference[0, 1:] = 1.0
    conference[1:, 0] = 1.0
    for row_pos in range(1, 14):
        for col_pos in range(1, 14):
            offset = (col_pos - row_pos) % 13
            if offset != 0:
                conference[row_pos, col_pos] = 1.0 if offset in squares_mod else -1.0
    kernel_first = np.array([[1.0, 1.0], [1.0, -1.0]])
    kernel_second = np.array([[1.0, -1.0], [-1.0, -1.0]])
    table = np.kron(conference, kernel_first) + np.kron(np.eye(14), kernel_second)
    return jnp.asarray(table / np.sqrt(28.0), jnp.float32)

def rotate(hidden):
    row_total = hidden.shape[0]
    precise = lax.Precision.HIGHEST
    values = hidden.astype(jnp.float32).reshape(row_total, 28, WALSH)
    values = jnp.einsum('ncp,pq->ncq', values, sylvester(WALSH), precision=precise)
    values = jnp.einsum('ncq,cb->nbq', values, paley_table(), precision=precise)
    return values.reshape(row_total, 28 * WALSH).astype(jnp.bfloat16)

def expand_rows(codes, scales):
    group_count = scales.shape[0]
    values = codes.astype(jnp.float32).reshape(group_count, codes.shape[0] // group_count, codes.shape[1])
    values = values * scales[:, None, :]
    return values.reshape(codes.shape).astype(jnp.bfloat16)

def expand_cols(codes, scales):
    group_count = scales.shape[1]
    values = codes.astype(jnp.float32).reshape(codes.shape[0], group_count, codes.shape[1] // group_count)
    values = values * scales[:, :, None]
    return values.reshape(codes.shape).astype(jnp.bfloat16)

def project_units(tokens, weight):
    return lax.dot_general(tokens, weight, (((1,), (1,)), ((), ())), preferred_element_type=jnp.float32)

def reference(tokens, gate_codes, gate_scales, up_codes, up_scales, down_codes, down_scales):
    gate = project_units(tokens, expand_cols(gate_codes, gate_scales))
    up_part = project_units(tokens, expand_cols(up_codes, up_scales))
    hidden = (jax.nn.silu(gate) * up_part).astype(jnp.bfloat16)
    rotated = rotate(hidden)
    summed = jnp.dot(rotated, expand_rows(down_codes, down_scales), preferred_element_type=jnp.float32)
    return summed.astype(jnp.bfloat16)
```

```python
import functools

import jax
import jax.numpy as jnp
import numpy as np
from jax import lax
from jax.experimental import pallas as pl
from jax.experimental.pallas import tpu as pltpu
from jax.sharding import PartitionSpec as P

MESH = pl.DeviceIdType.MESH
WALSH = 512
CHUNKS = 7
SKEW = 2
NORM = 1.0 / np.sqrt(28.0 * 512.0)
NT = (((1,), (1,)), ((), ()))


def sylvester_signs(order):
    table = np.ones((1, 1), np.float32)
    while table.shape[0] < order:
        table = np.kron(np.array([[1.0, 1.0], [1.0, -1.0]], np.float32), table)
    return table


def paley_signs():
    squares = {value * value % 13 for value in range(1, 13)}
    conference = np.zeros((14, 14))
    conference[0, 1:] = 1.0
    conference[1:, 0] = 1.0
    for row in range(1, 14):
        for col in range(1, 14):
            offset = (col - row) % 13
            if offset != 0:
                conference[row, col] = 1.0 if offset in squares else -1.0
    first = np.array([[1.0, 1.0], [1.0, -1.0]])
    second = np.array([[1.0, -1.0], [-1.0, -1.0]])
    return (np.kron(conference, first) + np.kron(np.eye(14), second)).astype(np.float32)


def row_of(core, chunk):
    return pl.multiple_of(jnp.where(chunk < 4, core * 64 + chunk * 16, 128 + core * 48 + (chunk - 4) * 16), 16)


def kernel(
    tokens_in, gate_in, gate_scale_in, up_in, up_scale_in, down_in, down_scale_in, signs_in, paley,
    out_ref,
    tok, codes, scales, dcodes, dscales, signs, weights, turned, pieces, gathered, mixed, hidden, final, partial, sums,
    load_sem, tok_s, tok_r, chain_s, chain_r, own_s, own_r, share_s, share_r, piece_s, piece_r, gath_s, gath_r,
    ring_s, ring_r, ringc_s, ringc_r, own_piece_s, own_piece_r, hid_s, hid_r, sum_s, sum_r,
):
    d, s, z = lax.axis_index("dp"), lax.axis_index("seq"), lax.axis_index("tensor")
    x, yh, c = s // 4, (s // 2) % 2, s % 2
    y = yh * 4 + d

    def at_y(row, core):
        return (row % 4, x * 4 + (row // 4) * 2 + core, z)

    sib = (d, s + 1 - 2 * c, z)
    x_peers = [(d, (s + 4 * k) % 16, z) for k in (1, 3, 2)]
    z_peers = [(d, s, (z + k) % 8) for k in range(1, 8)]
    y_up, y_down = at_y((y + 1) % 8, c), at_y((y + 7) % 8, c)
    y_opp = (y + 4) % 8
    opp, opp_sib = at_y(y_opp, c), at_y(y_opp, 1 - c)

    def remote(src, dst, ss, rs, dev):
        return pltpu.make_async_remote_copy(
            src_ref=src, dst_ref=dst, send_sem=ss, recv_sem=rs, device_id=dev, device_id_type=MESH
        )

    loads = [
        pltpu.make_async_copy(src, dst, load_sem.at[i])
        for i, (src, dst) in enumerate(
            [
                (tokens_in, tok.at[0]), (gate_in, codes.at[0]), (up_in, codes.at[1]), (gate_scale_in, scales.at[0]),
                (up_scale_in, scales.at[1]), (down_in, dcodes), (down_scale_in, dscales), (signs_in, signs),
            ]
        )
    ]
    for load in loads:
        load.start()
    barrier = pltpu.get_barrier_semaphore()
    peers = [sib, *x_peers, *z_peers, y_up, y_down, opp, opp_sib]
    for peer in peers:
        pl.semaphore_signal(barrier, inc=1, device_id=peer, device_id_type=MESH)
    pl.semaphore_wait(barrier, len(peers))

    loads[0].wait()
    tok_copies = [
        remote(tok.at[0], tok.at[slot], tok_s.at[i], tok_r.at[i], x_peers[i]) for i, slot in enumerate((2, 1, 3))
    ]
    for copy in tok_copies:
        copy.start()

    for load in loads[1:5]:
        load.wait()

    def chain(kind, chunk):
        last = (d == 3) if kind == 0 else (d == 0)
        half = jnp.where(last, 0, 1)
        rows = pl.ds(row_of(c, chunk), 16)
        return remote(
            weights.at[kind, half, rows, :], weights.at[kind, 1, rows, :],
            chain_s.at[kind, chunk], chain_r.at[kind, chunk], y_up if kind == 0 else y_down,
        )

    def own(kind, chunk):
        rows = pl.ds(row_of(c, chunk), 16)
        return remote(
            weights.at[kind, 0, rows, :], weights.at[kind, 0, rows, :],
            own_s.at[kind, chunk], own_r.at[kind, chunk], sib,
        )

    def share(kind, chunk):
        rows = pl.ds(row_of(c, chunk), 16)
        return remote(
            weights.at[kind, 1, rows, :], weights.at[kind, 1, rows, :],
            share_s.at[kind, chunk], share_r.at[kind, chunk], sib,
        )

    def expand(chunk, _):
        at = pl.multiple_of(chunk * 16, 16)
        row = row_of(c, chunk)
        for kind in range(2):
            scale = scales[kind, pl.ds(at, 16), :]
            for group in range(32):
                lanes = slice(group * 128, group * 128 + 128)
                value = codes[kind, pl.ds(at, 16), lanes].astype(jnp.float32) * scale[:, group : group + 1]
                weights[kind, 0, pl.ds(row, 16), lanes] = value.astype(jnp.bfloat16)

            @pl.when(d == (3 if kind == 0 else 0))
            def _():
                chain(kind, chunk).start()

            own(kind, chunk).start()
        return 0

    lax.fori_loop(0, CHUNKS, expand, 0)

    for load in loads[5:]:
        load.wait()
    for group in range(7):
        rows = slice(group * 128, group * 128 + 128)
        value = dcodes[rows, :].astype(jnp.float32) * dscales[group : group + 1, :]
        turned[:, rows] = value.astype(jnp.bfloat16).astype(jnp.float32).T.astype(jnp.bfloat16)

    own_lanes = pl.ds(pl.multiple_of((yh * 2 + c) * 896, 128), 896)

    def rows_for(row, core):
        return pl.ds(pl.multiple_of(row * 64 + core * 32, 32), 32)

    piece_copies = [
        remote(turned.at[rows, :], pieces.at[0, :, own_lanes], piece_s.at[i], piece_r.at[i], peer)
        for i, (rows, peer) in enumerate(
            [(rows_for(y, 1 - c), sib), (rows_for(y_opp, c), opp), (rows_for(y_opp, 1 - c), opp_sib)]
        )
    ]
    for copy in piece_copies:
        copy.start()
    pieces[0, :, own_lanes] = turned[rows_for(y, c), :]

    def steps(first, end):
        def body(n, _):
            for kind in range(2):
                hops = d if kind == 0 else 3 - d
                chunk = n - SKEW * hops

                @pl.when(jnp.logical_and(chunk >= 0, chunk < CHUNKS))
                def _():
                    chain(kind, chunk).wait_recv()

                    @pl.when(hops < 3)
                    def _():
                        chain(kind, chunk).start()

                    share(kind, chunk).start()

            return 0

        lax.fori_loop(first, end, body, 0)

    def wait_own(first, end):
        def body(chunk, _):
            for kind in range(2):
                own(kind, chunk).wait_recv()
            return 0

        lax.fori_loop(first, end, body, 0)

    def wait_share(first, end):
        def body(chunk, _):
            for kind in range(2):
                share(kind, chunk).wait_recv()
            return 0

        lax.fori_loop(first, end, body, 0)

    def units(half, rows, lane_tokens):
        gate = lax.dot_general(weights[0, half, rows, :], lane_tokens, NT, preferred_element_type=jnp.float32)
        up = lax.dot_general(weights[1, half, rows, :], lane_tokens, NT, preferred_element_type=jnp.float32)
        return (gate / (1.0 + jnp.exp(-gate)) * up).astype(jnp.bfloat16)

    def place(group, half, core, first, value):
        a = jnp.where(half == 0, yh, 1 - yh) * 2 + core
        rows = pl.ds(pl.multiple_of(z * 112 + first, 16), value.shape[0])
        hidden[group, a, rows, :] = value

    def spread(index, groups, half, first, count):
        pair = pl.ds(jnp.where(half == 0, yh, 1 - yh) * 2, 2)
        rows = pl.ds(pl.multiple_of(z * 112 + first, 16), count)
        block = hidden.at[groups, pair, rows, :]
        return [remote(block, block, hid_s.at[index, k], hid_r.at[index, k], z_peers[k]) for k in range(7)]

    def own_units(group):
        result = units(0, slice(0, 224), tok[2 * group : 2 * group + 2].reshape(128, 4096))
        for core in range(2):
            place(group, 0, core, 0, result[core * 64 : core * 64 + 64])
            place(group, 0, core, 64, result[128 + core * 48 : 176 + core * 48])
        copies = spread(group, pl.ds(group, 1), 0, 0, 112)
        for copy in copies:
            copy.start()
        return copies

    def other_units(index, first, count):
        result = units(1, slice(first * 2, first * 2 + count * 2), tok[...].reshape(256, 4096))
        for group in range(2):
            for core in range(2):
                place(group, 1, core, first, result[core * count : core * count + count, group * 128 : group * 128 + 128])
        copies = spread(index, pl.ds(0, 2), 1, first, count)
        for copy in copies:
            copy.start()
        return copies

    waits = list(piece_copies) + list(tok_copies)

    steps(0, 1)
    for copy in piece_copies:
        copy.wait_recv()
    gath_copies = [
        remote(pieces.at[0], pieces.at[slot], gath_s.at[i], gath_r.at[i], x_peers[i]) for i, slot in enumerate((2, 1, 3))
    ]
    for copy in gath_copies:
        copy.start()
    waits += gath_copies
    steps(1, 4)

    wait_own(0, CHUNKS)
    tok_copies[1].wait_recv()
    hid_copies = own_units(0)

    steps(4, 6)
    for copy in gath_copies:
        copy.wait_recv()
    for part in range(4):
        sums_of = [None] * 7
        for slot, offset in enumerate((0, 1, 3, 2)):
            for block in range(7):
                lanes = slice(block * 512 + part * 128, block * 512 + part * 128 + 128)
                value = pieces[slot, :, lanes].astype(jnp.float32)
                for i in range(7):
                    term = value * paley[((x + offset) % 4) * 7 + block, x * 7 + i]
                    sums_of[i] = term if sums_of[i] is None else sums_of[i] + term
        for i in range(7):
            mixed[i * 32 : i * 32 + 32, part * 128 : part * 128 + 128] = sums_of[i]
    high = mixed[...].astype(jnp.bfloat16)
    low = (mixed[...] - high.astype(jnp.float32)).astype(jnp.bfloat16)
    table = signs[...]
    rotated = jnp.dot(high, table, preferred_element_type=jnp.float32)
    rotated = (rotated + jnp.dot(low, table, preferred_element_type=jnp.float32)) * NORM
    my_rows = rows_for(y, c)
    for i in range(7):
        final[my_rows, i * 512 : i * 512 + 512] = rotated[i * 32 : i * 32 + 32].astype(jnp.bfloat16)

    def ring(way, step, half):
        row = (y + 8 - step) % 8 if way == 0 else (y + step) % 8
        block = final.at[rows_for(row, c), pl.ds(half * 1792, 1792)]
        return remote(
            block, block, ring_s.at[way, step, half], ring_r.at[way, step, half], y_up if way == 0 else y_down
        )

    def ring_core(way, step, half):
        row = (y + 7 - step) % 8 if way == 0 else (y + 1 + step) % 8
        block = final.at[rows_for(row, c), pl.ds(half * 1792, 1792)]
        return remote(block, block, ringc_s.at[way, step, half], ringc_r.at[way, step, half], sib)

    def halves(way, step):
        return (0, 1) if step < 3 else (way,)

    own_piece = remote(
        final.at[my_rows, :], final.at[my_rows, :], own_piece_s.at[0], own_piece_r.at[0], sib
    )
    for half in range(2):
        for way in range(2):
            ring(way, 0, half).start()
    own_piece.start()

    def ring_step(step):
        for half in range(2):
            for way in range(2):
                if half in halves(way, step):
                    ring(way, step, half).wait_recv()
                    if step < 3 and half in halves(way, step + 1):
                        ring(way, step + 1, half).start()
                    ring_core(way, step, half).start()

    steps(6, 8)
    tok_copies[0].wait_recv()
    tok_copies[2].wait_recv()
    hid_copies += own_units(1)
    steps(8, 10)
    wait_share(0, 4)
    hid_copies += other_units(2, 0, 64)
    ring_step(0)
    steps(10, CHUNKS + 3 * SKEW)
    wait_share(4, CHUNKS)
    hid_copies += other_units(3, 64, 48)
    for step in range(1, 4):
        ring_step(step)

    for copy in hid_copies:
        copy.wait_recv()
    own_piece.wait_recv()
    for step in range(4):
        for way in range(2):
            for half in halves(way, step):
                ring_core(way, step, half).wait_recv()

    for group in range(2):
        block = hidden[group].reshape(3584, 128)
        result = jnp.dot(final[...], block, preferred_element_type=jnp.float32).T
        partial[group * 128 : group * 128 + 128, :] = result.astype(jnp.bfloat16)
        if group == 0:
            total = result[:64]
    sum_copies = [
        remote(partial.at[pl.ds(64 * (i + 1), 64), :], sums.at[i], sum_s.at[i], sum_r.at[i], x_peers[i]) for i in range(3)
    ]
    for copy in sum_copies:
        copy.start()
    for copy in sum_copies:
        copy.wait_recv()
    for i in range(3):
        total = total + sums[i].astype(jnp.float32)
    out_ref[...] = total.astype(jnp.bfloat16)

    for copy in waits + hid_copies + sum_copies + [own_piece]:
        copy.wait_send()

    def end(chunk, _):
        for kind in range(2):
            chain(kind, chunk).wait_send()
            own(kind, chunk).wait_send()
            share(kind, chunk).wait_send()
        return 0

    lax.fori_loop(0, CHUNKS, end, 0)
    for step in range(4):
        for way in range(2):
            for half in halves(way, step):
                ring(way, step, half).wait_send()
                ring_core(way, step, half).wait_send()


def local(tokens, gate_codes, gate_scales, up_codes, up_scales, down_codes, down_scales):
    dma = pltpu.SemaphoreType.DMA
    bf16, f32 = jnp.bfloat16, jnp.float32
    anywhere = pl.BlockSpec(memory_space=pl.ANY)
    signs = jnp.asarray(sylvester_signs(WALSH), bf16)
    paley = jnp.asarray(paley_signs())
    return pl.pallas_call(
        kernel,
        out_shape=jax.ShapeDtypeStruct((64, 512), bf16),
        in_specs=[anywhere] * 8 + [pl.BlockSpec(memory_space=pltpu.SMEM)],
        out_specs=pl.BlockSpec(memory_space=pltpu.VMEM),
        scratch_shapes=[
            pltpu.VMEM((4, 64, 4096), bf16),
            pltpu.VMEM((2, 112, 4096), bf16),
            pltpu.VMEM((2, 112, 32), f32),
            pltpu.VMEM((896, 512), bf16),
            pltpu.VMEM((7, 512), f32),
            pltpu.VMEM((512, 512), bf16),
            pltpu.VMEM((2, 2, 224, 4096), bf16),
            pltpu.VMEM((512, 896), bf16),
            pltpu.VMEM((4, 32, 3584), bf16),
            pltpu.VMEM((8, 128), f32),
            pltpu.VMEM((224, 512), f32),
            pltpu.VMEM((2, 4, 896, 128), bf16),
            pltpu.VMEM((512, 3584), bf16),
            pltpu.VMEM((256, 512), bf16),
            pltpu.VMEM((3, 64, 512), bf16),
            dma((8,)),
            dma((3,)), dma((3,)),
            dma((2, CHUNKS)), dma((2, CHUNKS)),
            dma((2, CHUNKS)), dma((2, CHUNKS)),
            dma((2, CHUNKS)), dma((2, CHUNKS)),
            dma((3,)), dma((3,)),
            dma((3,)), dma((3,)),
            dma((2, 4, 2)), dma((2, 4, 2)),
            dma((2, 4, 2)), dma((2, 4, 2)),
            dma((1,)), dma((1,)),
            dma((4, 7)), dma((4, 7)),
            dma((3,)), dma((3,)),
        ],
        compiler_params=pltpu.CompilerParams(
            collective_id=0, has_side_effects=True, vmem_limit_bytes=56 * 1024 * 1024
        ),
        cost_estimate=pl.CostEstimate(flops=4 * 10**9, bytes_accessed=4 * 10**6, transcendentals=10**5),
        name="feed_forward",
    )(tokens, gate_codes, gate_scales, up_codes, up_scales, down_codes, down_scales, signs, paley)


def solution(mesh):
    return jax.shard_map(
        local,
        mesh=mesh,
        in_specs=(
            P(("dp", "seq"), None),
            P(("seq", "tensor"), None),
            P(("seq", "tensor"), None),
            P(("seq", "tensor"), None),
            P(("seq", "tensor"), None),
            P("seq", "tensor"),
            P("seq", "tensor"),
        ),
        out_specs=P(("dp", "seq"), "tensor"),
        check_vma=False,
    )
```

```python
import functools

import jax
import jax.numpy as jnp
import numpy as np
from jax import lax
from jax.experimental import pallas as pl
from jax.experimental.pallas import tpu as pltpu
from jax.sharding import PartitionSpec as P

MESH = pl.DeviceIdType.MESH
WALSH = 512
CHUNKS = 7
PARTS = 2
WIDTH = 4096 // PARTS
SKEW = 3
STEPS = CHUNKS * PARTS + 3 * SKEW
GROUPS = ((0, 32), (32, 32), (64, 32), (96, 16))
NORM = 1.0 / np.sqrt(28.0 * 512.0)
NT = (((1,), (1,)), ((), ()))


def sylvester_signs(order):
    table = np.ones((1, 1), np.float32)
    while table.shape[0] < order:
        table = np.kron(np.array([[1.0, 1.0], [1.0, -1.0]], np.float32), table)
    return table


def paley_signs():
    squares = {value * value % 13 for value in range(1, 13)}
    conference = np.zeros((14, 14))
    conference[0, 1:] = 1.0
    conference[1:, 0] = 1.0
    for row in range(1, 14):
        for col in range(1, 14):
            offset = (col - row) % 13
            if offset != 0:
                conference[row, col] = 1.0 if offset in squares else -1.0
    first = np.array([[1.0, 1.0], [1.0, -1.0]])
    second = np.array([[1.0, -1.0], [-1.0, -1.0]])
    return (np.kron(conference, first) + np.kron(np.eye(14), second)).astype(np.float32)


def row_of(core, chunk):
    return pl.multiple_of(jnp.where(chunk < 6, chunk // 2 * 64 + core * 32 + chunk % 2 * 16, 192 + core * 16), 16)


def kernel(
    tokens_in, gate_in, gate_scale_in, up_in, up_scale_in, down_in, down_scale_in, signs_in, paley,
    out_ref,
    tok, codes, scales, dcodes, dscales, signs, weights, turned, turned_scales, pieces, mixed, hidden, final, early, partial, sums,
    load_sem, tok_s, tok_r, tokf_s, tokf_r, chain_s, chain_r, own_s, own_r, share_s, share_r, piece_s, piece_r, gath_s, gath_r, gathf_s, gathf_r,
    ring_s, ring_r, ringc_s, ringc_r, own_piece_s, own_piece_r, hid_s, hid_r, sum_s, sum_r,
):
    d, s, z = lax.axis_index("dp"), lax.axis_index("seq"), lax.axis_index("tensor")
    x, yh, c = s // 4, (s // 2) % 2, s % 2
    y = yh * 4 + d

    def at_y(row, core):
        return (row % 4, x * 4 + (row // 4) * 2 + core, z)

    sib = (d, s + 1 - 2 * c, z)
    x_peers = [(d, (s + 4 * k) % 16, z) for k in (1, 3, 2)]
    z_peers = [(d, s, (z + k) % 8) for k in range(1, 8)]
    y_up, y_down = at_y((y + 1) % 8, c), at_y((y + 7) % 8, c)
    y_opp = (y + 4) % 8
    opp, opp_sib = at_y(y_opp, c), at_y(y_opp, 1 - c)

    def remote(src, dst, ss, rs, dev):
        return pltpu.make_async_remote_copy(
            src_ref=src, dst_ref=dst, send_sem=ss, recv_sem=rs, device_id=dev, device_id_type=MESH
        )

    loads = [
        pltpu.make_async_copy(src, dst, load_sem.at[i])
        for i, (src, dst) in enumerate(
            [
                (tokens_in, tok.at[0]), (gate_in, codes.at[0]), (up_in, codes.at[1]), (gate_scale_in, scales.at[0]),
                (up_scale_in, scales.at[1]), (down_in, dcodes), (down_scale_in, dscales), (signs_in, signs),
            ]
        )
    ]
    for load in loads:
        load.start()
    barrier = pltpu.get_barrier_semaphore()
    peers = [sib, *x_peers, *z_peers, y_up, y_down, opp, opp_sib]
    for peer in peers:
        pl.semaphore_signal(barrier, inc=1, device_id=peer, device_id_type=MESH)
    pl.semaphore_wait(barrier, len(peers))

    x_up, x_down, x_far = x_peers

    def tok_copy(way, half):
        rows = pl.ds(half * 32, 32)
        return remote(
            tok.at[0, rows], tok.at[2 - way, rows], tok_s.at[way, half], tok_r.at[way, half], (x_up, x_down)[way]
        )

    def tok_forward(way):
        rows = pl.ds(way * 32, 32)
        return remote(tok.at[2 - way, rows], tok.at[3, rows], tokf_s.at[way], tokf_r.at[way], (x_up, x_down)[way])

    def gath_copy(way, half):
        rows = pl.ds(half * 16, 16)
        return remote(
            pieces.at[0, rows], pieces.at[2 - way, rows], gath_s.at[way, half], gath_r.at[way, half],
            (x_up, x_down)[way],
        )

    def gath_forward(way):
        rows = pl.ds(way * 16, 16)
        return remote(
            pieces.at[2 - way, rows], pieces.at[3, rows], gathf_s.at[way], gathf_r.at[way], (x_up, x_down)[way]
        )

    loads[0].wait()
    for order in range(2):
        for way in range(2):
            tok_copy(way, way if order == 0 else 1 - way).start()

    for load in loads[5:]:
        load.wait()
    for group in range(7):
        rows = slice(group * 128, group * 128 + 128)
        value = dcodes[rows, :].astype(jnp.float32) * dscales[group : group + 1, :]
        turned[:, rows] = value.astype(jnp.bfloat16).astype(jnp.float32).T.astype(jnp.bfloat16)

    own_lanes = pl.ds(pl.multiple_of((yh * 2 + c) * 896, 128), 896)

    def rows_for(row, core):
        return pl.ds(pl.multiple_of(row * 64 + core * 32, 32), 32)

    piece_copies = [
        remote(turned.at[rows, :], pieces.at[0, :, own_lanes], piece_s.at[i], piece_r.at[i], peer)
        for i, (rows, peer) in enumerate(
            [(rows_for(y, 1 - c), sib), (rows_for(y_opp, c), opp), (rows_for(y_opp, 1 - c), opp_sib)]
        )
    ]
    for copy in piece_copies:
        copy.start()
    pieces[0, :, own_lanes] = turned[rows_for(y, c), :]

    for load in loads[1:5]:
        load.wait()

    def chain(kind, index):
        last = (d == 3) if kind == 0 else (d == 0)
        half = jnp.where(last, 0, 1)
        rows = pl.ds(row_of(c, index // PARTS), 16)
        lanes = pl.ds(pl.multiple_of(index % PARTS * WIDTH, WIDTH), WIDTH)
        return remote(
            weights.at[kind, half, rows, lanes], weights.at[kind, 1, rows, lanes],
            chain_s.at[kind, index], chain_r.at[kind, index], y_up if kind == 0 else y_down,
        )

    def own(kind, chunk):
        rows = pl.ds(row_of(c, chunk), 16)
        return remote(
            weights.at[kind, 0, rows, :], weights.at[kind, 0, rows, :],
            own_s.at[kind, chunk], own_r.at[kind, chunk], sib,
        )

    def share(kind, index):
        rows = pl.ds(row_of(c, index // PARTS), 16)
        lanes = pl.ds(pl.multiple_of(index % PARTS * WIDTH, WIDTH), WIDTH)
        block = weights.at[kind, 1, rows, lanes]
        return remote(block, block, share_s.at[kind, index], share_r.at[kind, index], sib)

    for kind in range(2):
        turned_scales[kind] = scales[kind].T

    def expand(chunk, _):
        at = pl.multiple_of(chunk * 16, 16)
        row = row_of(c, chunk)
        for kind in range(2):
            scale = turned_scales[kind, pl.ds(at, 16), :]
            for group in range(32):
                lanes = slice(group * 128, group * 128 + 128)
                value = codes[kind, pl.ds(at, 16), lanes].astype(jnp.float32) * scale[:, group : group + 1]
                weights[kind, 0, pl.ds(row, 16), lanes] = value.astype(jnp.bfloat16)

            @pl.when(d == (3 if kind == 0 else 0))
            def _():
                for part in range(PARTS):
                    chain(kind, chunk * PARTS + part).start()

            own(kind, chunk).start()
        return 0

    lax.fori_loop(0, CHUNKS, expand, 0)

    def steps(first, end):
        def body(n, _):
            for kind in range(2):
                hops = d if kind == 0 else 3 - d
                index = n - SKEW * hops

                @pl.when(jnp.logical_and(index >= 0, index < CHUNKS * PARTS))
                def _():
                    chain(kind, index).wait_recv()

                    @pl.when(hops < 3)
                    def _():
                        chain(kind, index).start()

                    share(kind, index).start()

            return 0

        lax.fori_loop(first, end, body, 0)

    def wait_each(copy, first, end):
        def body(index, _):
            for kind in range(2):
                copy(kind, index).wait_recv()
            return 0

        lax.fori_loop(first, end, body, 0)

    def units(half, rows, lane_tokens):
        gate = lax.dot_general(weights[0, half, rows, :], lane_tokens, NT, preferred_element_type=jnp.float32)
        up = lax.dot_general(weights[1, half, rows, :], lane_tokens, NT, preferred_element_type=jnp.float32)
        return (gate / (1.0 + jnp.exp(-gate)) * up).astype(jnp.bfloat16)

    def place(group, half, core, first, value):
        a = jnp.where(half == 0, yh, 1 - yh) * 2 + core
        rows = pl.ds(pl.multiple_of(z * 112 + first, 16), value.shape[0])
        hidden[group, a, rows, :] = value

    def block_of(groups, half, first, count, origin, core=None):
        a = jnp.where(half == 0, yh, 1 - yh) * 2
        rows = pl.ds(pl.multiple_of(lax.rem(z + origin, 8) * 112 + first, 16), count)
        return hidden.at[groups, pl.ds(a, 2) if core is None else pl.ds(a + core, 1), rows, :]

    class Spread:
        def __init__(self, index, groups, half, first, count, direct=False):
            self.index, self.where = index, (groups, half, first, count)
            places = (1, 7, 2, 6, 3, 5, 4) if direct else (1, 7, 2, 6)
            self.sent = [self.copy(i, 0, place) for i, place in enumerate(places)]
            self.direct, self.seen = direct, set()
            for copy in self.sent:
                copy.start()

        def copy(self, slot, origin, place, core=None):
            block = block_of(*self.where, origin, core)
            return remote(
                block, block, hid_s.at[self.index, slot], hid_r.at[self.index, slot], (d, s, lax.rem(z + place, 8))
            )

        def relay(self):
            for way, (origin, near, far) in enumerate(((6, 1, 2), (2, 7, 6))):
                self.sent[2 + way].wait_recv()
                more = [self.copy(4 + way, origin, near), self.copy(6 + way, origin, far, way)]
                for copy in more:
                    copy.start()
                self.sent += more

        def wait(self):
            for i, copy in enumerate(self.sent):
                if self.direct or i not in (2, 3):
                    copy.wait_recv()

    def own_units(group):
        result = units(0, slice(0, 224), tok[2 * group : 2 * group + 2].reshape(128, 4096))
        for first, count in GROUPS:
            for core in range(2):
                place(group, 0, core, first, result[2 * first + core * count : 2 * first + core * count + count])
        return Spread(group, pl.ds(group, 1), 0, 0, 112)

    def other_units(index):
        first, count = GROUPS[index]
        result = units(1, slice(first * 2, first * 2 + count * 2), tok[...].reshape(256, 4096))
        for group in range(2):
            for core in range(2):
                part = result[core * count : core * count + count, group * 128 : group * 128 + 128]
                place(group, 1, core, first, part)
        return Spread(2 + index, pl.ds(0, 2), 1, first, count, direct=index == 3)

    my_rows = rows_for(y, c)

    def ring(way, step, half):
        row = (y + 8 - step) % 8 if way == 0 else (y + step) % 8
        block = final.at[rows_for(row, c), pl.ds(half * 1792, 1792)]
        return remote(
            block, block, ring_s.at[way, step, half], ring_r.at[way, step, half], y_up if way == 0 else y_down
        )

    def ring_core(way, step, half):
        row = (y + 7 - step) % 8 if way == 0 else (y + 1 + step) % 8
        block = final.at[rows_for(row, c), pl.ds(half * 1792, 1792)]
        return remote(block, block, ringc_s.at[way, step, half], ringc_r.at[way, step, half], sib)

    def halves(way, step):
        return (0, 1) if step < 3 else (way,)

    own_piece = remote(final.at[my_rows, :], final.at[my_rows, :], own_piece_s.at[0], own_piece_r.at[0], sib)

    def ring_step(step):
        for half in range(2):
            for way in range(2):
                if half in halves(way, step):
                    ring(way, step, half).wait_recv()
                    if step < 3 and half in halves(way, step + 1):
                        ring(way, step + 1, half).start()
                    ring_core(way, step, half).start()

    def rotate():
        for part in range(4):
            sums_of = [None] * 7
            for slot, offset in enumerate((0, 1, 3, 2)):
                for block in range(7):
                    lanes = slice(block * 512 + part * 128, block * 512 + part * 128 + 128)
                    value = pieces[slot, :, lanes].astype(jnp.float32)
                    for i in range(7):
                        term = value * paley[((x + offset) % 4) * 7 + block, x * 7 + i]
                        sums_of[i] = term if sums_of[i] is None else sums_of[i] + term
            for i in range(7):
                mixed[i * 32 : i * 32 + 32, part * 128 : part * 128 + 128] = sums_of[i]
        high = mixed[...].astype(jnp.bfloat16)
        low = (mixed[...] - high.astype(jnp.float32)).astype(jnp.bfloat16)
        table = signs[...]
        rotated = jnp.dot(high, table, preferred_element_type=jnp.float32)
        rotated = (rotated + jnp.dot(low, table, preferred_element_type=jnp.float32)) * NORM
        for i in range(7):
            final[my_rows, i * 512 : i * 512 + 512] = rotated[i * 32 : i * 32 + 32].astype(jnp.bfloat16)

    steps(0, 2)
    for way in range(2):
        tok_copy(way, way).wait_recv()
        tok_forward(way).start()
    steps(2, 4)
    for copy in piece_copies:
        copy.wait_recv()
    for order in range(2):
        for way in range(2):
            gath_copy(way, way if order == 0 else 1 - way).start()
    steps(4, 6)
    wait_each(own, 0, CHUNKS)
    tok_copy(1, 0).wait_recv()
    spreads = [own_units(0)]
    steps(6, 8)
    for way in range(2):
        gath_copy(way, way).wait_recv()
        gath_forward(way).start()
    steps(8, 9)
    tok_copy(0, 1).wait_recv()
    for way in range(2):
        tok_forward(way).wait_recv()
    spreads[0].relay()
    spreads.append(own_units(1))
    steps(9, 11)
    for way in range(2):
        gath_copy(way, 1 - way).wait_recv()
        gath_forward(way).wait_recv()
    rotate()
    for half in range(2):
        for way in range(2):
            ring(way, 0, half).start()
    own_piece.start()
    steps(11, 13)
    spreads[1].relay()
    wait_each(share, 0, 2 * PARTS)
    spreads.append(other_units(0))
    steps(13, 17)
    wait_each(share, 2 * PARTS, 4 * PARTS)
    spreads.append(other_units(1))
    ring_step(0)
    spreads[2].relay()
    steps(17, 21)
    wait_each(share, 4 * PARTS, 6 * PARTS)
    spreads.append(other_units(2))
    spreads[3].relay()
    ring_step(1)
    steps(21, STEPS)
    wait_each(share, 6 * PARTS, 7 * PARTS)
    spreads.append(other_units(3))
    spreads[4].relay()
    ring_step(2)
    ring_step(3)

    own_piece.wait_recv()
    for step in range(4):
        for way in range(2):
            for half in halves(way, step):
                ring_core(way, step, half).wait_recv()

    def down(group, half):
        a = (yh if half == 0 else 1 - yh) * 2
        lanes = pl.ds(pl.multiple_of(a * 896, 128), 1792)
        block = hidden[group, pl.ds(a, 2)].reshape(1792, 128)
        return jnp.dot(final[:, lanes], block, preferred_element_type=jnp.float32)

    sum_copies = [
        remote(partial.at[pl.ds(64 * (i + 1), 64), :], sums.at[i], sum_s.at[i], sum_r.at[i], x_peers[i]) for i in range(3)
    ]
    spreads[0].wait()
    spreads[1].wait()
    for group in range(2):
        early[group] = down(group, 0)
    for spread in spreads[2:]:
        spread.wait()
    result = (early[1] + down(1, 1)).T
    partial[128:256, :] = result.astype(jnp.bfloat16)
    sum_copies[2].start()
    sum_copies[1].start()
    result = (early[0] + down(0, 1)).T
    partial[64:128, :] = result[64:].astype(jnp.bfloat16)
    sum_copies[0].start()
    total = result[:64]
    for copy in sum_copies:
        copy.wait_recv()
    for i in range(3):
        total = total + sums[i].astype(jnp.float32)
    out_ref[...] = total.astype(jnp.bfloat16)

    for copy in piece_copies + sum_copies + [own_piece]:
        copy.wait_send()
    for spread in spreads:
        for copy in spread.sent:
            copy.wait_send()
    for way in range(2):
        for half in range(2):
            tok_copy(way, half).wait_send()
            gath_copy(way, half).wait_send()
        tok_forward(way).wait_send()
        gath_forward(way).wait_send()

    def end(index, _):
        for kind in range(2):
            chain(kind, index).wait_send()
            share(kind, index).wait_send()
        return 0

    def end_own(chunk, _):
        for kind in range(2):
            own(kind, chunk).wait_send()
        return 0

    lax.fori_loop(0, CHUNKS * PARTS, end, 0)
    lax.fori_loop(0, CHUNKS, end_own, 0)
    for step in range(4):
        for way in range(2):
            for half in halves(way, step):
                ring(way, step, half).wait_send()
                ring_core(way, step, half).wait_send()


def local(tokens, gate_codes, gate_scales, up_codes, up_scales, down_codes, down_scales):
    dma = pltpu.SemaphoreType.DMA
    bf16, f32 = jnp.bfloat16, jnp.float32
    anywhere = pl.BlockSpec(memory_space=pl.ANY)
    signs = jnp.asarray(sylvester_signs(WALSH), bf16)
    paley = jnp.asarray(paley_signs())
    return pl.pallas_call(
        kernel,
        out_shape=jax.ShapeDtypeStruct((64, 512), bf16),
        in_specs=[anywhere] * 8 + [pl.BlockSpec(memory_space=pltpu.SMEM)],
        out_specs=pl.BlockSpec(memory_space=pltpu.VMEM),
        scratch_shapes=[
            pltpu.VMEM((4, 64, 4096), bf16),
            pltpu.VMEM((2, 112, 4096), bf16),
            pltpu.VMEM((2, 32, 112), f32),
            pltpu.VMEM((896, 512), bf16),
            pltpu.VMEM((7, 512), f32),
            pltpu.VMEM((512, 512), bf16),
            pltpu.VMEM((2, 2, 224, 4096), bf16),
            pltpu.VMEM((512, 896), bf16),
            pltpu.VMEM((2, 112, 32), f32),
            pltpu.VMEM((4, 32, 3584), bf16),
            pltpu.VMEM((224, 512), f32),
            pltpu.VMEM((2, 4, 896, 128), bf16),
            pltpu.VMEM((512, 3584), bf16),
            pltpu.VMEM((2, 512, 128), f32),
            pltpu.VMEM((256, 512), bf16),
            pltpu.VMEM((3, 64, 512), bf16),
            dma((8,)),
            dma((2, 2)), dma((2, 2)),
            dma((2,)), dma((2,)),
            dma((2, CHUNKS * PARTS)), dma((2, CHUNKS * PARTS)),
            dma((2, CHUNKS)), dma((2, CHUNKS)),
            dma((2, CHUNKS * PARTS)), dma((2, CHUNKS * PARTS)),
            dma((3,)), dma((3,)),
            dma((2, 2)), dma((2, 2)),
            dma((2,)), dma((2,)),
            dma((2, 4, 2)), dma((2, 4, 2)),
            dma((2, 4, 2)), dma((2, 4, 2)),
            dma((1,)), dma((1,)),
            dma((6, 8)), dma((6, 8)),
            dma((3,)), dma((3,)),
        ],
        compiler_params=pltpu.CompilerParams(
            collective_id=0, has_side_effects=True, vmem_limit_bytes=56 * 1024 * 1024
        ),
        cost_estimate=pl.CostEstimate(flops=4 * 10**9, bytes_accessed=4 * 10**6, transcendentals=10**5),
        name="feed_forward",
    )(tokens, gate_codes, gate_scales.T, up_codes, up_scales.T, down_codes, down_scales, signs, paley)


def solution(mesh):
    return jax.shard_map(
        local,
        mesh=mesh,
        in_specs=(
            P(("dp", "seq"), None),
            P(("seq", "tensor"), None),
            P(("seq", "tensor"), None),
            P(("seq", "tensor"), None),
            P(("seq", "tensor"), None),
            P("seq", "tensor"),
            P("seq", "tensor"),
        ),
        out_specs=P(("dp", "seq"), "tensor"),
        check_vma=False,
    )
```

```python
import functools

import jax
import jax.numpy as jnp
import numpy as np
from jax import lax
from jax.experimental import pallas as pl
from jax.experimental.pallas import tpu as pltpu
from jax.sharding import PartitionSpec as P

MESH = pl.DeviceIdType.MESH
WALSH = 512
CHUNKS = 7
PARTS = 2
WIDTH = 4096 // PARTS
SKEW = 3
STEPS = CHUNKS * PARTS + 3 * SKEW
GROUPS = ((0, 32), (32, 32), (64, 32), (96, 16))
NORM = 1.0 / np.sqrt(28.0 * 512.0)
NT = (((1,), (1,)), ((), ()))


def sylvester_signs(order):
    table = np.ones((1, 1), np.float32)
    while table.shape[0] < order:
        table = np.kron(np.array([[1.0, 1.0], [1.0, -1.0]], np.float32), table)
    return table


def paley_signs():
    squares = {value * value % 13 for value in range(1, 13)}
    conference = np.zeros((14, 14))
    conference[0, 1:] = 1.0
    conference[1:, 0] = 1.0
    for row in range(1, 14):
        for col in range(1, 14):
            offset = (col - row) % 13
            if offset != 0:
                conference[row, col] = 1.0 if offset in squares else -1.0
    first = np.array([[1.0, 1.0], [1.0, -1.0]])
    second = np.array([[1.0, -1.0], [-1.0, -1.0]])
    return (np.kron(conference, first) + np.kron(np.eye(14), second)).astype(np.float32)


def row_of(core, chunk):
    return pl.multiple_of(jnp.where(chunk < 6, chunk // 2 * 64 + core * 32 + chunk % 2 * 16, 192 + core * 16), 16)


def kernel(
    tokens_in, gate_in, gate_scale_in, up_in, up_scale_in, down_in, down_scale_in, signs_in, paley,
    out_ref,
    tok, codes, scales, dcodes, dscales, signs, weights, turned, turned_scales, pieces, mixed, hidden, final, early, partial, sums,
    load_sem, tok_s, tok_r, tokf_s, tokf_r, chain_s, chain_r, own_s, own_r, share_s, share_r, piece_s, piece_r, gath_s, gath_r,
    ring_s, ring_r, ringc_s, ringc_r, own_piece_s, own_piece_r, hid_s, hid_r, sum_s, sum_r,
):
    d, s, z = lax.axis_index("dp"), lax.axis_index("seq"), lax.axis_index("tensor")
    x, yh, c = s // 4, (s // 2) % 2, s % 2
    y = yh * 4 + d

    def at_y(row, core):
        return (row % 4, x * 4 + (row // 4) * 2 + core, z)

    sib = (d, s + 1 - 2 * c, z)
    x_peers = [(d, (s + 4 * k) % 16, z) for k in (1, 3, 2)]
    z_peers = [(d, s, (z + k) % 8) for k in range(1, 8)]
    y_up, y_down = at_y((y + 1) % 8, c), at_y((y + 7) % 8, c)
    y_opp = (y + 4) % 8
    opp, opp_sib = at_y(y_opp, c), at_y(y_opp, 1 - c)

    def remote(src, dst, ss, rs, dev):
        return pltpu.make_async_remote_copy(
            src_ref=src, dst_ref=dst, send_sem=ss, recv_sem=rs, device_id=dev, device_id_type=MESH
        )

    loads = [
        pltpu.make_async_copy(src, dst, load_sem.at[i])
        for i, (src, dst) in enumerate(
            [
                (tokens_in, tok.at[0]), (gate_in, codes.at[0]), (up_in, codes.at[1]), (gate_scale_in, scales.at[0]),
                (up_scale_in, scales.at[1]), (down_in, dcodes), (down_scale_in, dscales), (signs_in, signs),
            ]
        )
    ]
    for load in loads:
        load.start()
    barrier = pltpu.get_barrier_semaphore()
    peers = [sib, *x_peers, *z_peers, y_up, y_down, opp, opp_sib]
    for peer in peers:
        pl.semaphore_signal(barrier, inc=1, device_id=peer, device_id_type=MESH)

    x_up, x_down, x_far = x_peers

    def tok_copy(way, half):
        rows = pl.ds(half * 32, 32)
        return remote(
            tok.at[0, rows], tok.at[2 - way, rows], tok_s.at[way, half], tok_r.at[way, half], (x_up, x_down)[way]
        )

    def tok_forward(way):
        rows = pl.ds(way * 32, 32)
        return remote(tok.at[2 - way, rows], tok.at[3, rows], tokf_s.at[way], tokf_r.at[way], (x_up, x_down)[way])

    def gath_copy(half, peer):
        lanes = pl.ds(pl.multiple_of(jnp.where(half == 0, yh, 1 - yh) * 1792, 128), 1792)
        return remote(
            pieces.at[0, :, lanes], pieces.at[(2, 1, 3)[peer], :, lanes],
            gath_s.at[half, peer], gath_r.at[half, peer], x_peers[peer],
        )

    for load in loads[5:]:
        load.wait()
    for group in range(7):
        rows = slice(group * 128, group * 128 + 128)
        value = dcodes[rows, :].astype(jnp.float32) * dscales[group : group + 1, :]
        turned[:, rows] = value.astype(jnp.bfloat16).astype(jnp.float32).T.astype(jnp.bfloat16)

    own_lanes = pl.ds(pl.multiple_of((yh * 2 + c) * 896, 128), 896)

    def rows_for(row, core):
        return pl.ds(pl.multiple_of(row * 64 + core * 32, 32), 32)

    piece_copies = [
        remote(turned.at[rows, :], pieces.at[0, :, own_lanes], piece_s.at[i], piece_r.at[i], peer)
        for i, (rows, peer) in enumerate(
            [(rows_for(y, 1 - c), sib), (rows_for(y_opp, c), opp), (rows_for(y_opp, 1 - c), opp_sib)]
        )
    ]
    pieces[0, :, own_lanes] = turned[rows_for(y, c), :]

    for load in loads[1:5]:
        load.wait()

    def chain(kind, index):
        last = (d == 3) if kind == 0 else (d == 0)
        half = jnp.where(last, 0, 1)
        rows = pl.ds(row_of(c, index // PARTS), 16)
        lanes = pl.ds(pl.multiple_of(index % PARTS * WIDTH, WIDTH), WIDTH)
        return remote(
            weights.at[kind, half, rows, lanes], weights.at[kind, 1, rows, lanes],
            chain_s.at[kind, index], chain_r.at[kind, index], y_up if kind == 0 else y_down,
        )

    def own(kind, chunk):
        rows = pl.ds(row_of(c, chunk), 16)
        return remote(
            weights.at[kind, 0, rows, :], weights.at[kind, 0, rows, :],
            own_s.at[kind, chunk], own_r.at[kind, chunk], sib,
        )

    def share(kind, index):
        rows = pl.ds(row_of(c, index // PARTS), 16)
        lanes = pl.ds(pl.multiple_of(index % PARTS * WIDTH, WIDTH), WIDTH)
        block = weights.at[kind, 1, rows, lanes]
        return remote(block, block, share_s.at[kind, index], share_r.at[kind, index], sib)

    for kind in range(2):
        turned_scales[kind] = scales[kind].T

    def expand(chunk, _):
        at = pl.multiple_of(chunk * 16, 16)
        row = row_of(c, chunk)
        for kind in range(2):
            scale = turned_scales[kind, pl.ds(at, 16), :]
            for group in range(32):
                lanes = slice(group * 128, group * 128 + 128)
                value = codes[kind, pl.ds(at, 16), lanes].astype(jnp.float32) * scale[:, group : group + 1]
                weights[kind, 0, pl.ds(row, 16), lanes] = value.astype(jnp.bfloat16)
        return 0

    lax.fori_loop(0, CHUNKS, expand, 0)
    loads[0].wait()

    pl.semaphore_wait(barrier, len(peers))
    for copy in piece_copies:
        copy.start()
    for way in range(2):
        tok_copy(way, way).start()

    def first_hop(index, _):
        for kind in range(2):

            @pl.when(d == (3 if kind == 0 else 0))
            def _():
                chain(kind, index).start()

        return 0

    def to_core(chunk, _):
        for kind in range(2):
            own(kind, chunk).start()
        return 0

    lax.fori_loop(0, CHUNKS * PARTS, first_hop, 0)
    lax.fori_loop(0, CHUNKS, to_core, 0)

    def steps(first, end):
        def body(n, _):
            for kind in range(2):
                hops = d if kind == 0 else 3 - d
                index = n - SKEW * hops

                @pl.when(jnp.logical_and(index >= 0, index < CHUNKS * PARTS))
                def _():
                    chain(kind, index).wait_recv()

                    @pl.when(hops < 3)
                    def _():
                        chain(kind, index).start()

                    share(kind, index).start()

            return 0

        lax.fori_loop(first, end, body, 0)

    def wait_each(copy, first, end):
        def body(index, _):
            for kind in range(2):
                copy(kind, index).wait_recv()
            return 0

        lax.fori_loop(first, end, body, 0)

    def units(half, rows, lane_tokens):
        gate = lax.dot_general(weights[0, half, rows, :], lane_tokens, NT, preferred_element_type=jnp.float32)
        up = lax.dot_general(weights[1, half, rows, :], lane_tokens, NT, preferred_element_type=jnp.float32)
        return (gate / (1.0 + jnp.exp(-gate)) * up).astype(jnp.bfloat16)

    def place(group, half, core, first, value):
        a = jnp.where(half == 0, yh, 1 - yh) * 2 + core
        rows = pl.ds(pl.multiple_of(z * 112 + first, 16), value.shape[0])
        hidden[group, a, rows, :] = value

    def block_of(groups, half, first, count, origin, core=None):
        a = jnp.where(half == 0, yh, 1 - yh) * 2
        rows = pl.ds(pl.multiple_of(lax.rem(z + origin, 8) * 112 + first, 16), count)
        return hidden.at[groups, pl.ds(a, 2) if core is None else pl.ds(a + core, 1), rows, :]

    class Spread:
        def __init__(self, index, groups, half, first, count, direct=False):
            self.index, self.where = index, (groups, half, first, count)
            places = (1, 7, 2, 6, 3, 5, 4) if direct else (1, 7, 2, 6)
            self.sent = [self.copy(i, 0, place) for i, place in enumerate(places)]
            self.direct, self.seen = direct, set()
            for copy in self.sent:
                copy.start()

        def copy(self, slot, origin, place, core=None):
            block = block_of(*self.where, origin, core)
            return remote(
                block, block, hid_s.at[self.index, slot], hid_r.at[self.index, slot], (d, s, lax.rem(z + place, 8))
            )

        def relay(self):
            for way, (origin, near, far) in enumerate(((6, 1, 2), (2, 7, 6))):
                self.sent[2 + way].wait_recv()
                more = [self.copy(4 + way, origin, near), self.copy(6 + way, origin, far, way)]
                for copy in more:
                    copy.start()
                self.sent += more

        def wait(self):
            for i, copy in enumerate(self.sent):
                if self.direct or i not in (2, 3):
                    copy.wait_recv()

    def own_units(group, index):
        first, count = GROUPS[index]
        lane_tokens = tok[2 * group : 2 * group + 2].reshape(128, 4096)
        result = units(0, slice(first * 2, first * 2 + count * 2), lane_tokens)
        for core in range(2):
            place(group, 0, core, first, result[core * count : core * count + count])

    def own_spread(group):
        return Spread(group, pl.ds(group, 1), 0, 0, 112)

    def other_units(index):
        first, count = GROUPS[index]
        result = units(1, slice(first * 2, first * 2 + count * 2), tok[...].reshape(256, 4096))
        for group in range(2):
            for core in range(2):
                part = result[core * count : core * count + count, group * 128 : group * 128 + 128]
                place(group, 1, core, first, part)
        return Spread(2 + index, pl.ds(0, 2), 1, first, count, direct=index == 3)

    my_rows = rows_for(y, c)

    def ring(way, step, half):
        row = (y + 8 - step) % 8 if way == 0 else (y + step) % 8
        block = final.at[rows_for(row, c), pl.ds(half * 1792, 1792)]
        return remote(
            block, block, ring_s.at[way, step, half], ring_r.at[way, step, half], y_up if way == 0 else y_down
        )

    def ring_core(way, step, half):
        row = (y + 7 - step) % 8 if way == 0 else (y + 1 + step) % 8
        block = final.at[rows_for(row, c), pl.ds(half * 1792, 1792)]
        return remote(block, block, ringc_s.at[way, step, half], ringc_r.at[way, step, half], sib)

    def halves(way, step):
        return (0, 1) if step < 3 else (way,)

    own_piece = remote(final.at[my_rows, :], final.at[my_rows, :], own_piece_s.at[0], own_piece_r.at[0], sib)

    def ring_step(step):
        for half in range(2):
            for way in range(2):
                if half in halves(way, step):
                    ring(way, step, half).wait_recv()
                    if step < 3 and half in halves(way, step + 1):
                        ring(way, step + 1, half).start()
                    ring_core(way, step, half).start()

    def mix(part):
        sums_of = [None] * 7
        for slot, offset in enumerate((0, 1, 3, 2)):
            for block in range(7):
                lanes = slice(block * 512 + part * 128, block * 512 + part * 128 + 128)
                value = pieces[slot, :, lanes].astype(jnp.float32)
                for i in range(7):
                    term = value * paley[((x + offset) % 4) * 7 + block, x * 7 + i]
                    sums_of[i] = term if sums_of[i] is None else sums_of[i] + term
        for i in range(7):
            mixed[i * 32 : i * 32 + 32, part * 128 : part * 128 + 128] = sums_of[i]

    def rotate():
        high = mixed[...].astype(jnp.bfloat16)
        low = (mixed[...] - high.astype(jnp.float32)).astype(jnp.bfloat16)
        table = signs[...]
        rotated = jnp.dot(high, table, preferred_element_type=jnp.float32)
        rotated = (rotated + jnp.dot(low, table, preferred_element_type=jnp.float32)) * NORM
        for i in range(7):
            final[my_rows, i * 512 : i * 512 + 512] = rotated[i * 32 : i * 32 + 32].astype(jnp.bfloat16)

    spreads = [None] * 6
    piece_copies[0].wait_recv()
    for peer in (2, 0, 1):
        gath_copy(0, peer).start()
    steps(0, 2)
    piece_copies[1].wait_recv()
    piece_copies[2].wait_recv()
    for peer in (2, 0, 1):
        gath_copy(1, peer).start()
    for way in range(2):
        tok_copy(way, 1 - way).start()
    steps(2, 5)
    for way in range(2):
        tok_copy(way, way).wait_recv()
        tok_forward(way).start()
    steps(5, 7)
    for half in range(2):
        for peer in range(3):
            gath_copy(half, peer).wait_recv()
    mix(0)
    mix(1)
    steps(7, 8)
    mix(2)
    mix(3)
    rotate()
    for half in range(2):
        for way in range(2):
            ring(way, 0, half).start()
    own_piece.start()
    wait_each(own, 0, CHUNKS)
    tok_copy(1, 0).wait_recv()
    own_units(0, 0)
    steps(8, 9)
    own_units(0, 1)
    steps(9, 10)
    own_units(0, 2)
    steps(10, 11)
    own_units(0, 3)
    spreads[0] = own_spread(0)
    steps(11, 13)
    tok_copy(0, 1).wait_recv()
    for way in range(2):
        tok_forward(way).wait_recv()
    own_units(1, 0)
    steps(13, 14)
    own_units(1, 1)
    spreads[0].relay()
    steps(14, 15)
    own_units(1, 2)
    steps(15, 16)
    own_units(1, 3)
    spreads[1] = own_spread(1)
    ring_step(0)
    steps(16, 17)
    wait_each(share, 0 * PARTS, 2 * PARTS)
    spreads[2] = other_units(0)
    steps(17, 18)
    spreads[1].relay()
    steps(18, 19)
    wait_each(share, 2 * PARTS, 4 * PARTS)
    spreads[3] = other_units(1)
    spreads[2].relay()
    steps(19, 20)
    ring_step(1)
    steps(20, 21)
    wait_each(share, 4 * PARTS, 6 * PARTS)
    spreads[4] = other_units(2)
    spreads[3].relay()
    steps(21, 23)
    wait_each(share, 6 * PARTS, 7 * PARTS)
    spreads[5] = other_units(3)
    ring_step(2)
    spreads[4].relay()
    ring_step(3)

    own_piece.wait_recv()
    for step in range(4):
        for way in range(2):
            for half in halves(way, step):
                ring_core(way, step, half).wait_recv()

    def down(group, half):
        a = (yh if half == 0 else 1 - yh) * 2
        lanes = pl.ds(pl.multiple_of(a * 896, 128), 1792)
        block = hidden[group, pl.ds(a, 2)].reshape(1792, 128)
        return jnp.dot(final[:, lanes], block, preferred_element_type=jnp.float32)

    sum_copies = [
        remote(partial.at[pl.ds(64 * (i + 1), 64), :], sums.at[i], sum_s.at[i], sum_r.at[i], x_peers[i]) for i in range(3)
    ]
    spreads[0].wait()
    spreads[1].wait()
    for group in range(2):
        early[group] = down(group, 0)
    for spread in spreads[2:]:
        spread.wait()
    result = (early[1] + down(1, 1)).T
    partial[128:256, :] = result.astype(jnp.bfloat16)
    sum_copies[2].start()
    sum_copies[1].start()
    result = (early[0] + down(0, 1)).T
    partial[64:128, :] = result[64:].astype(jnp.bfloat16)
    sum_copies[0].start()
    total = result[:64]
    for copy in sum_copies:
        copy.wait_recv()
    for i in range(3):
        total = total + sums[i].astype(jnp.float32)
    out_ref[...] = total.astype(jnp.bfloat16)

    for copy in piece_copies + sum_copies + [own_piece]:
        copy.wait_send()
    for spread in spreads:
        for copy in spread.sent:
            copy.wait_send()
    for way in range(2):
        for half in range(2):
            tok_copy(way, half).wait_send()
        tok_forward(way).wait_send()
        for peer in range(3):
            gath_copy(way, peer).wait_send()

    def end(index, _):
        for kind in range(2):
            chain(kind, index).wait_send()
            share(kind, index).wait_send()
        return 0

    def end_own(chunk, _):
        for kind in range(2):
            own(kind, chunk).wait_send()
        return 0

    lax.fori_loop(0, CHUNKS * PARTS, end, 0)
    lax.fori_loop(0, CHUNKS, end_own, 0)
    for step in range(4):
        for way in range(2):
            for half in halves(way, step):
                ring(way, step, half).wait_send()
                ring_core(way, step, half).wait_send()


def local(tokens, gate_codes, gate_scales, up_codes, up_scales, down_codes, down_scales):
    dma = pltpu.SemaphoreType.DMA
    bf16, f32 = jnp.bfloat16, jnp.float32
    anywhere = pl.BlockSpec(memory_space=pl.ANY)
    signs = jnp.asarray(sylvester_signs(WALSH), bf16)
    paley = jnp.asarray(paley_signs())
    return pl.pallas_call(
        kernel,
        out_shape=jax.ShapeDtypeStruct((64, 512), bf16),
        in_specs=[anywhere] * 8 + [pl.BlockSpec(memory_space=pltpu.SMEM)],
        out_specs=pl.BlockSpec(memory_space=pltpu.VMEM),
        scratch_shapes=[
            pltpu.VMEM((4, 64, 4096), bf16),
            pltpu.VMEM((2, 112, 4096), bf16),
            pltpu.VMEM((2, 32, 112), f32),
            pltpu.VMEM((896, 512), bf16),
            pltpu.VMEM((7, 512), f32),
            pltpu.VMEM((512, 512), bf16),
            pltpu.VMEM((2, 2, 224, 4096), bf16),
            pltpu.VMEM((512, 896), bf16),
            pltpu.VMEM((2, 112, 32), f32),
            pltpu.VMEM((4, 32, 3584), bf16),
            pltpu.VMEM((224, 512), f32),
            pltpu.VMEM((2, 4, 896, 128), bf16),
            pltpu.VMEM((512, 3584), bf16),
            pltpu.VMEM((2, 512, 128), f32),
            pltpu.VMEM((256, 512), bf16),
            pltpu.VMEM((3, 64, 512), bf16),
            dma((8,)),
            dma((2, 2)), dma((2, 2)),
            dma((2,)), dma((2,)),
            dma((2, CHUNKS * PARTS)), dma((2, CHUNKS * PARTS)),
            dma((2, CHUNKS)), dma((2, CHUNKS)),
            dma((2, CHUNKS * PARTS)), dma((2, CHUNKS * PARTS)),
            dma((3,)), dma((3,)),
            dma((2, 3)), dma((2, 3)),
            dma((2, 4, 2)), dma((2, 4, 2)),
            dma((2, 4, 2)), dma((2, 4, 2)),
            dma((1,)), dma((1,)),
            dma((6, 8)), dma((6, 8)),
            dma((3,)), dma((3,)),
        ],
        compiler_params=pltpu.CompilerParams(
            collective_id=0, has_side_effects=True, vmem_limit_bytes=56 * 1024 * 1024
        ),
        cost_estimate=pl.CostEstimate(flops=4 * 10**9, bytes_accessed=4 * 10**6, transcendentals=10**5),
        name="feed_forward",
    )(tokens, gate_codes, gate_scales.T, up_codes, up_scales.T, down_codes, down_scales, signs, paley)


def solution(mesh):
    return jax.shard_map(
        local,
        mesh=mesh,
        in_specs=(
            P(("dp", "seq"), None),
            P(("seq", "tensor"), None),
            P(("seq", "tensor"), None),
            P(("seq", "tensor"), None),
            P(("seq", "tensor"), None),
            P("seq", "tensor"),
            P("seq", "tensor"),
        ),
        out_specs=P(("dp", "seq"), "tensor"),
        check_vma=False,
    )
```

```python
import functools

import jax
import jax.numpy as jnp
import numpy as np
from jax import lax
from jax.experimental import pallas as pl
from jax.experimental.pallas import tpu as pltpu
from jax.sharding import PartitionSpec as P

MESH = pl.DeviceIdType.MESH
WALSH = 512
CHUNKS = 7
PARTS = 2
WIDTH = 4096 // PARTS
SKEW = 3
STEPS = CHUNKS * PARTS + 3 * SKEW
GROUPS = ((0, 32), (32, 32), (64, 32), (96, 16))
NORM = 1.0 / np.sqrt(28.0 * 512.0)
NT = (((1,), (1,)), ((), ()))


def sylvester_signs(order):
    table = np.ones((1, 1), np.float32)
    while table.shape[0] < order:
        table = np.kron(np.array([[1.0, 1.0], [1.0, -1.0]], np.float32), table)
    return table


def paley_signs():
    squares = {value * value % 13 for value in range(1, 13)}
    conference = np.zeros((14, 14))
    conference[0, 1:] = 1.0
    conference[1:, 0] = 1.0
    for row in range(1, 14):
        for col in range(1, 14):
            offset = (col - row) % 13
            if offset != 0:
                conference[row, col] = 1.0 if offset in squares else -1.0
    first = np.array([[1.0, 1.0], [1.0, -1.0]])
    second = np.array([[1.0, -1.0], [-1.0, -1.0]])
    return (np.kron(conference, first) + np.kron(np.eye(14), second)).astype(np.float32)


def row_of(core, chunk):
    return pl.multiple_of(jnp.where(chunk < 6, chunk // 2 * 64 + core * 32 + chunk % 2 * 16, 192 + core * 16), 16)


def kernel(
    tokens_in, gate_in, gate_scale_in, up_in, up_scale_in, down_in, down_scale_in, signs_in, paley,
    out_ref,
    tok, codes, scales, dcodes, dscales, signs, weights, turned, turned_scales, pieces, mixed, hidden, final, early, partial, sums,
    load_sem, tok_s, tok_r, tokf_s, tokf_r, chain_s, chain_r, own_s, own_r, share_s, share_r, piece_s, piece_r, gath_s, gath_r,
    ring_s, ring_r, ringc_s, ringc_r, own_piece_s, own_piece_r, hid_s, hid_r, sum_s, sum_r,
):
    d, s, z = lax.axis_index("dp"), lax.axis_index("seq"), lax.axis_index("tensor")
    x, yh, c = s // 4, (s // 2) % 2, s % 2
    y = yh * 4 + d

    def at_y(row, core):
        return (row % 4, x * 4 + (row // 4) * 2 + core, z)

    sib = (d, s + 1 - 2 * c, z)
    x_peers = [(d, (s + 4 * k) % 16, z) for k in (1, 3, 2)]
    z_peers = [(d, s, (z + k) % 8) for k in range(1, 8)]
    y_up, y_down = at_y((y + 1) % 8, c), at_y((y + 7) % 8, c)
    y_opp = (y + 4) % 8
    opp, opp_sib = at_y(y_opp, c), at_y(y_opp, 1 - c)

    def remote(src, dst, ss, rs, dev):
        return pltpu.make_async_remote_copy(
            src_ref=src, dst_ref=dst, send_sem=ss, recv_sem=rs, device_id=dev, device_id_type=MESH
        )

    loads = [
        pltpu.make_async_copy(src, dst, load_sem.at[i])
        for i, (src, dst) in enumerate(
            [
                (tokens_in, tok.at[0]), (gate_in, codes.at[0]), (up_in, codes.at[1]), (gate_scale_in, scales.at[0]),
                (up_scale_in, scales.at[1]), (down_in, dcodes), (down_scale_in, dscales), (signs_in, signs),
            ]
        )
    ]
    for load in loads:
        load.start()
    barrier = pltpu.get_barrier_semaphore()
    peers = [sib, *x_peers, *z_peers, y_up, y_down, opp, opp_sib]
    for peer in peers:
        pl.semaphore_signal(barrier, inc=1, device_id=peer, device_id_type=MESH)

    x_up, x_down, x_far = x_peers

    def tok_copy(way, half):
        rows = pl.ds(half * 32, 32)
        return remote(
            tok.at[0, rows], tok.at[2 - way, rows], tok_s.at[way, half], tok_r.at[way, half], (x_up, x_down)[way]
        )

    def tok_forward(way):
        rows = pl.ds(way * 32, 32)
        return remote(tok.at[2 - way, rows], tok.at[3, rows], tokf_s.at[way], tokf_r.at[way], (x_up, x_down)[way])

    def gath_copy(half, peer):
        lanes = pl.ds(pl.multiple_of(jnp.where(half == 0, yh, 1 - yh) * 1792, 128), 1792)
        return remote(
            pieces.at[0, :, lanes], pieces.at[(2, 1, 3)[peer], :, lanes],
            gath_s.at[half, peer], gath_r.at[half, peer], x_peers[peer],
        )

    for load in loads[5:]:
        load.wait()
    for group in range(7):
        rows = slice(group * 128, group * 128 + 128)
        value = dcodes[rows, :].astype(jnp.float32) * dscales[group : group + 1, :]
        turned[:, rows] = value.astype(jnp.bfloat16).astype(jnp.float32).T.astype(jnp.bfloat16)

    own_lanes = pl.ds(pl.multiple_of((yh * 2 + c) * 896, 128), 896)

    def rows_for(row, core):
        return pl.ds(pl.multiple_of(row * 64 + core * 32, 32), 32)

    piece_copies = [
        remote(turned.at[rows, :], pieces.at[0, :, own_lanes], piece_s.at[i], piece_r.at[i], peer)
        for i, (rows, peer) in enumerate(
            [(rows_for(y, 1 - c), sib), (rows_for(y_opp, c), opp), (rows_for(y_opp, 1 - c), opp_sib)]
        )
    ]
    pieces[0, :, own_lanes] = turned[rows_for(y, c), :]

    for load in loads[1:5]:
        load.wait()

    def chain(kind, index):
        last = (d == 3) if kind == 0 else (d == 0)
        half = jnp.where(last, 0, 1)
        rows = pl.ds(row_of(c, index // PARTS), 16)
        lanes = pl.ds(pl.multiple_of(index % PARTS * WIDTH, WIDTH), WIDTH)
        return remote(
            weights.at[kind, half, rows, lanes], weights.at[kind, 1, rows, lanes],
            chain_s.at[kind, index], chain_r.at[kind, index], y_up if kind == 0 else y_down,
        )

    def own(kind, chunk):
        rows = pl.ds(row_of(c, chunk), 16)
        return remote(
            weights.at[kind, 0, rows, :], weights.at[kind, 0, rows, :],
            own_s.at[kind, chunk], own_r.at[kind, chunk], sib,
        )

    def share(kind, index):
        rows = pl.ds(row_of(c, index // PARTS), 16)
        lanes = pl.ds(pl.multiple_of(index % PARTS * WIDTH, WIDTH), WIDTH)
        block = weights.at[kind, 1, rows, lanes]
        return remote(block, block, share_s.at[kind, index], share_r.at[kind, index], sib)

    for kind in range(2):
        turned_scales[kind] = scales[kind].T

    def expand(chunk, _):
        at = pl.multiple_of(chunk * 16, 16)
        row = row_of(c, chunk)
        for kind in range(2):
            scale = turned_scales[kind, pl.ds(at, 16), :]
            for group in range(32):
                lanes = slice(group * 128, group * 128 + 128)
                value = codes[kind, pl.ds(at, 16), lanes].astype(jnp.float32) * scale[:, group : group + 1]
                weights[kind, 0, pl.ds(row, 16), lanes] = value.astype(jnp.bfloat16)
        return 0

    lax.fori_loop(0, CHUNKS, expand, 0)
    loads[0].wait()

    pl.semaphore_wait(barrier, len(peers))
    for copy in piece_copies:
        copy.start()
    for way in range(2):
        tok_copy(way, way).start()

    def first_hop(index, _):
        for kind in range(2):

            @pl.when(d == (3 if kind == 0 else 0))
            def _():
                chain(kind, index).start()

        return 0

    def to_core(chunk, _):
        for kind in range(2):
            own(kind, chunk).start()
        return 0

    lax.fori_loop(0, CHUNKS * PARTS, first_hop, 0)
    lax.fori_loop(0, CHUNKS, to_core, 0)

    def steps(first, end):
        def body(n, _):
            for kind in range(2):
                hops = d if kind == 0 else 3 - d
                index = n - SKEW * hops

                @pl.when(jnp.logical_and(index >= 0, index < CHUNKS * PARTS))
                def _():
                    chain(kind, index).wait_recv()

                    @pl.when(hops < 3)
                    def _():
                        chain(kind, index).start()

                    share(kind, index).start()

            return 0

        lax.fori_loop(first, end, body, 0)

    def wait_each(copy, first, end):
        def body(index, _):
            for kind in range(2):
                copy(kind, index).wait_recv()
            return 0

        lax.fori_loop(first, end, body, 0)

    def units(half, rows, lane_tokens):
        gate = lax.dot_general(weights[0, half, rows, :], lane_tokens, NT, preferred_element_type=jnp.float32)
        up = lax.dot_general(weights[1, half, rows, :], lane_tokens, NT, preferred_element_type=jnp.float32)
        return (gate / (1.0 + jnp.exp(-gate)) * up).astype(jnp.bfloat16)

    def place(group, half, core, first, value):
        a = jnp.where(half == 0, yh, 1 - yh) * 2 + core
        rows = pl.ds(pl.multiple_of(z * 112 + first, 16), value.shape[0])
        hidden[group, a, rows, :] = value

    def block_of(groups, half, first, count, origin, core=None):
        a = jnp.where(half == 0, yh, 1 - yh) * 2
        rows = pl.ds(pl.multiple_of(lax.rem(z + origin, 8) * 112 + first, 16), count)
        return hidden.at[groups, pl.ds(a, 2) if core is None else pl.ds(a + core, 1), rows, :]

    class Spread:
        def __init__(self, index, groups, half, first, count, direct=False):
            self.index, self.where = index, (groups, half, first, count)
            places = (1, 7, 2, 6, 3, 5, 4) if direct else (1, 7, 2, 6)
            self.sent = [self.copy(i, 0, place) for i, place in enumerate(places)]
            self.direct, self.seen = direct, set()
            for copy in self.sent:
                copy.start()

        def copy(self, slot, origin, place, core=None):
            block = block_of(*self.where, origin, core)
            return remote(
                block, block, hid_s.at[self.index, slot], hid_r.at[self.index, slot], (d, s, lax.rem(z + place, 8))
            )

        def relay(self):
            for way, (origin, near, far) in enumerate(((6, 1, 2), (2, 7, 6))):
                self.sent[2 + way].wait_recv()
                more = [self.copy(4 + way, origin, near), self.copy(6 + way, origin, far, way)]
                for copy in more:
                    copy.start()
                self.sent += more

        def wait(self):
            for i, copy in enumerate(self.sent):
                if self.direct or i not in (2, 3):
                    copy.wait_recv()

    def own_units(group, index):
        first, count = GROUPS[index]
        lane_tokens = tok[2 * group : 2 * group + 2].reshape(128, 4096)
        result = units(0, slice(first * 2, first * 2 + count * 2), lane_tokens)
        for core in range(2):
            place(group, 0, core, first, result[core * count : core * count + count])

    def own_spread(group):
        return Spread(group, pl.ds(group, 1), 0, 0, 112)

    def other_units(index):
        first, count = GROUPS[index]
        result = units(1, slice(first * 2, first * 2 + count * 2), tok[...].reshape(256, 4096))
        for group in range(2):
            for core in range(2):
                part = result[core * count : core * count + count, group * 128 : group * 128 + 128]
                place(group, 1, core, first, part)
        return Spread(2 + index, pl.ds(0, 2), 1, first, count, direct=index == 3)

    my_rows = rows_for(y, c)

    def ring(way, step, half):
        row = (y + 8 - step) % 8 if way == 0 else (y + step) % 8
        block = final.at[rows_for(row, c), pl.ds(half * 1792, 1792)]
        return remote(
            block, block, ring_s.at[way, step, half], ring_r.at[way, step, half], y_up if way == 0 else y_down
        )

    def ring_core(way, step, half):
        row = (y + 7 - step) % 8 if way == 0 else (y + 1 + step) % 8
        block = final.at[rows_for(row, c), pl.ds(half * 1792, 1792)]
        return remote(block, block, ringc_s.at[way, step, half], ringc_r.at[way, step, half], sib)

    def halves(way, step):
        return (0, 1) if step < 3 else (way,)

    own_piece = remote(final.at[my_rows, :], final.at[my_rows, :], own_piece_s.at[0], own_piece_r.at[0], sib)

    def ring_step(step):
        for half in range(2):
            for way in range(2):
                if half in halves(way, step):
                    ring(way, step, half).wait_recv()
                    if step < 3 and half in halves(way, step + 1):
                        ring(way, step + 1, half).start()
                    ring_core(way, step, half).start()

    def mix(part):
        sums_of = [None] * 7
        for slot, offset in enumerate((0, 1, 3, 2)):
            for block in range(7):
                lanes = slice(block * 512 + part * 128, block * 512 + part * 128 + 128)
                value = pieces[slot, :, lanes].astype(jnp.float32)
                for i in range(7):
                    term = value * paley[((x + offset) % 4) * 7 + block, x * 7 + i]
                    sums_of[i] = term if sums_of[i] is None else sums_of[i] + term
        for i in range(7):
            mixed[i * 32 : i * 32 + 32, part * 128 : part * 128 + 128] = sums_of[i]

    def rotate():
        high = mixed[...].astype(jnp.bfloat16)
        low = (mixed[...] - high.astype(jnp.float32)).astype(jnp.bfloat16)
        table = signs[...]
        rotated = jnp.dot(high, table, preferred_element_type=jnp.float32)
        rotated = (rotated + jnp.dot(low, table, preferred_element_type=jnp.float32)) * NORM
        for i in range(7):
            final[my_rows, i * 512 : i * 512 + 512] = rotated[i * 32 : i * 32 + 32].astype(jnp.bfloat16)

    spreads = [None] * 6
    piece_copies[0].wait_recv()
    for peer in (2, 0, 1):
        gath_copy(0, peer).start()
    steps(0, 2)
    piece_copies[1].wait_recv()
    piece_copies[2].wait_recv()
    for peer in (2, 0, 1):
        gath_copy(1, peer).start()
    for way in range(2):
        tok_copy(way, 1 - way).start()
    steps(2, 5)
    for way in range(2):
        tok_copy(way, way).wait_recv()
        tok_forward(way).start()
    steps(5, 7)
    for half in range(2):
        for peer in range(3):
            gath_copy(half, peer).wait_recv()
    mix(0)
    mix(1)
    mix(2)
    mix(3)
    rotate()
    for half in range(2):
        for way in range(2):
            ring(way, 0, half).start()
    own_piece.start()
    steps(7, 8)
    wait_each(own, 0, CHUNKS)
    tok_copy(1, 0).wait_recv()
    own_units(0, 0)
    steps(8, 9)
    own_units(0, 1)
    steps(9, 10)
    own_units(0, 2)
    steps(10, 11)
    own_units(0, 3)
    spreads[0] = own_spread(0)
    steps(11, 13)
    tok_copy(0, 1).wait_recv()
    for way in range(2):
        tok_forward(way).wait_recv()
    own_units(1, 0)
    steps(13, 14)
    own_units(1, 1)
    spreads[0].relay()
    steps(14, 15)
    own_units(1, 2)
    steps(15, 16)
    own_units(1, 3)
    spreads[1] = own_spread(1)
    ring_step(0)
    steps(16, 17)
    wait_each(share, 0 * PARTS, 2 * PARTS)
    spreads[2] = other_units(0)
    steps(17, 18)
    spreads[1].relay()
    steps(18, 19)
    wait_each(share, 2 * PARTS, 4 * PARTS)
    spreads[3] = other_units(1)
    spreads[2].relay()
    steps(19, 20)
    ring_step(1)
    steps(20, 21)
    wait_each(share, 4 * PARTS, 6 * PARTS)
    spreads[4] = other_units(2)
    spreads[3].relay()
    steps(21, 23)
    ring_step(2)
    wait_each(share, 6 * PARTS, 7 * PARTS)
    spreads[5] = other_units(3)
    spreads[4].relay()
    ring_step(3)

    own_piece.wait_recv()
    for step in range(4):
        for way in range(2):
            for half in halves(way, step):
                ring_core(way, step, half).wait_recv()

    def down(group, half):
        a = (yh if half == 0 else 1 - yh) * 2
        lanes = pl.ds(pl.multiple_of(a * 896, 128), 1792)
        block = hidden[group, pl.ds(a, 2)].reshape(1792, 128)
        return jnp.dot(final[:, lanes], block, preferred_element_type=jnp.float32)

    sum_copies = [
        remote(partial.at[pl.ds(64 * (i + 1), 64), :], sums.at[i], sum_s.at[i], sum_r.at[i], x_peers[i]) for i in range(3)
    ]
    spreads[0].wait()
    spreads[1].wait()
    for group in range(2):
        early[group] = down(group, 0)
    for spread in spreads[2:]:
        spread.wait()
    result = (early[1] + down(1, 1)).T
    partial[128:256, :] = result.astype(jnp.bfloat16)
    sum_copies[2].start()
    sum_copies[1].start()
    result = (early[0] + down(0, 1)).T
    partial[64:128, :] = result[64:].astype(jnp.bfloat16)
    sum_copies[0].start()
    total = result[:64]
    for copy in sum_copies:
        copy.wait_recv()
    for i in range(3):
        total = total + sums[i].astype(jnp.float32)
    out_ref[...] = total.astype(jnp.bfloat16)

    for copy in piece_copies + sum_copies + [own_piece]:
        copy.wait_send()
    for spread in spreads:
        for copy in spread.sent:
            copy.wait_send()
    for way in range(2):
        for half in range(2):
            tok_copy(way, half).wait_send()
        tok_forward(way).wait_send()
        for peer in range(3):
            gath_copy(way, peer).wait_send()

    def end(index, _):
        for kind in range(2):
            chain(kind, index).wait_send()
            share(kind, index).wait_send()
        return 0

    def end_own(chunk, _):
        for kind in range(2):
            own(kind, chunk).wait_send()
        return 0

    lax.fori_loop(0, CHUNKS * PARTS, end, 0)
    lax.fori_loop(0, CHUNKS, end_own, 0)
    for step in range(4):
        for way in range(2):
            for half in halves(way, step):
                ring(way, step, half).wait_send()
                ring_core(way, step, half).wait_send()


def local(tokens, gate_codes, gate_scales, up_codes, up_scales, down_codes, down_scales):
    dma = pltpu.SemaphoreType.DMA
    bf16, f32 = jnp.bfloat16, jnp.float32
    anywhere = pl.BlockSpec(memory_space=pl.ANY)
    signs = jnp.asarray(sylvester_signs(WALSH), bf16)
    paley = jnp.asarray(paley_signs())
    return pl.pallas_call(
        kernel,
        out_shape=jax.ShapeDtypeStruct((64, 512), bf16),
        in_specs=[anywhere] * 8 + [pl.BlockSpec(memory_space=pltpu.SMEM)],
        out_specs=pl.BlockSpec(memory_space=pltpu.VMEM),
        scratch_shapes=[
            pltpu.VMEM((4, 64, 4096), bf16),
            pltpu.VMEM((2, 112, 4096), bf16),
            pltpu.VMEM((2, 32, 112), f32),
            pltpu.VMEM((896, 512), bf16),
            pltpu.VMEM((7, 512), f32),
            pltpu.VMEM((512, 512), bf16),
            pltpu.VMEM((2, 2, 224, 4096), bf16),
            pltpu.VMEM((512, 896), bf16),
            pltpu.VMEM((2, 112, 32), f32),
            pltpu.VMEM((4, 32, 3584), bf16),
            pltpu.VMEM((224, 512), f32),
            pltpu.VMEM((2, 4, 896, 128), bf16),
            pltpu.VMEM((512, 3584), bf16),
            pltpu.VMEM((2, 512, 128), f32),
            pltpu.VMEM((256, 512), bf16),
            pltpu.VMEM((3, 64, 512), bf16),
            dma((8,)),
            dma((2, 2)), dma((2, 2)),
            dma((2,)), dma((2,)),
            dma((2, CHUNKS * PARTS)), dma((2, CHUNKS * PARTS)),
            dma((2, CHUNKS)), dma((2, CHUNKS)),
            dma((2, CHUNKS * PARTS)), dma((2, CHUNKS * PARTS)),
            dma((3,)), dma((3,)),
            dma((2, 3)), dma((2, 3)),
            dma((2, 4, 2)), dma((2, 4, 2)),
            dma((2, 4, 2)), dma((2, 4, 2)),
            dma((1,)), dma((1,)),
            dma((6, 8)), dma((6, 8)),
            dma((3,)), dma((3,)),
        ],
        compiler_params=pltpu.CompilerParams(
            collective_id=0, has_side_effects=True, vmem_limit_bytes=56 * 1024 * 1024
        ),
        cost_estimate=pl.CostEstimate(flops=4 * 10**9, bytes_accessed=4 * 10**6, transcendentals=10**5),
        name="feed_forward",
    )(tokens, gate_codes, gate_scales.T, up_codes, up_scales.T, down_codes, down_scales, signs, paley)


def solution(mesh):
    return jax.shard_map(
        local,
        mesh=mesh,
        in_specs=(
            P(("dp", "seq"), None),
            P(("seq", "tensor"), None),
            P(("seq", "tensor"), None),
            P(("seq", "tensor"), None),
            P(("seq", "tensor"), None),
            P("seq", "tensor"),
            P("seq", "tensor"),
        ),
        out_specs=P(("dp", "seq"), "tensor"),
        check_vma=False,
    )
```
